512 devices in a mesh: rep: 16 (over y, z_lo), head: 32 (over z_hi, x, core).
Axes of the slice: x: 4, y: 8, z: 8 (z_hi: 4, z_lo: 2; z = z_hi * 2 + z_lo), core: 2. Of those that a mesh axis runs over, the one named last changes fastest.
Arguments:
- step_hidden: bfloat16 [80, 12288], P(None, 'rep')
- paused_hidden: bfloat16 [1792, 12288], P('head', 'rep')
- ln_gain: float32 [12288], P('rep'), may hold values from 0.1 to 1.9
- ln_bias: float32 [12288], P('rep'), may hold values from -3 to 3
- w_query: bfloat16 [12288, 8192], P('rep', 'head')
- w_keyval: bfloat16 [12288, 2, 8192], P('rep', None, 'head'), may hold values from -0.0546875 to 0.0546875
- w_out: bfloat16 [8192, 12288], P('head', 'rep'), may hold values from -0.5 to 0.5
- cache: bfloat16 [64, 2, 512, 8192], P('rep', None, None, 'head'), may hold values from -6 to 6
- cache_lengths: int32 [64], P('rep'), may hold values from 1 to 512, as said below
- partner: int32 [16], replicated, may hold values from 0 to 15, each once
- paused_count: int32 [16], replicated, may hold values from 1 to 112, as said below
Outputs:
- paused_keyval: bfloat16 [1792, 2, 8192], P('rep', None, 'head')
- attention_update: bfloat16 [80, 12288], P(None, 'rep')
The draws below stay inside these ranges and needn't reach their ends.
Inputs may be any that keep to these rules, and one draw needn't show every extreme that they name: `cache_lengths`: every resident sequence has at least one valid slot; some sequence fills all 512. `partner`: A permutation of the sequence groups. `paused_count`: some group's paused sequence fills all 112 slots.
All inputs are finite; a program needn't handle non-finite values.
Results may differ from the reference program's by a relative error of at most 0.012.
The reference program's roundings to bfloat16 on the way (of `normed_step`, `normed_paused`, `received`, `query`, `step_keyval`, `weights` and `mixed`) count: a program that leaves them out, or rounds other values in their place, can miss the bound.
Values may be sent and summed in bfloat16 or wider, within the bound.
A program may use at most 64 MiB of HBM per device.

```python
import math
import jax
import jax.numpy as jnp
from jax import lax

D = 12288
HEADS = 64
HEAD_DIM = 128
SEQ_DEV = 4
CACHE = 512
MIG = 112
NQ = 5
SEQS = 64
ROWS = 80
PAUSED = 1792
WIDTH = 8192
N_REP = 16


def rough_hidden(key, count):
    first = jax.random.fold_in(key, 0)
    columns = 0.6 * jnp.power(3.0, jnp.arange(D, dtype=jnp.float32) / D)
    values = jax.random.normal(first, (count, D), jnp.float32) * columns
    return values.astype(jnp.bfloat16)


def draw_step_hidden(key, part):
    key = jax.random.fold_in(key, 11)
    return rough_hidden(key, ROWS)


def draw_paused_hidden(key, part):
    key = jax.random.fold_in(key, 12)
    return rough_hidden(key, PAUSED)


def draw_w_query(key, part):
    key = jax.random.fold_in(key, 13)
    first = jax.random.fold_in(key, 0)
    values = jax.random.normal(first, (D, WIDTH), jnp.float32) / math.sqrt(D)
    return values.astype(jnp.bfloat16)


def draw_cache_lengths(key, part):
    key = jax.random.fold_in(key, 14)
    first, second = jax.random.split(key)
    lengths = jax.random.randint(first, (SEQS,), 1, CACHE + 1, dtype=jnp.int32)
    place = jax.random.randint(second, (), 0, SEQS, dtype=jnp.int32)
    return lengths.at[place].set(CACHE)


def draw_paused_count(key, part):
    key = jax.random.fold_in(key, 15)
    first, second = jax.random.split(key)
    counts = jax.random.randint(first, (N_REP,), 1, MIG + 1, dtype=jnp.int32)
    place = jax.random.randint(second, (), 0, N_REP, dtype=jnp.int32)
    return counts.at[place].set(MIG)


def shard_levels(key, dims, shards, least, high):
    factor_of = 1.0
    for dim, blocks in shards:
        heights = jax.random.uniform(jax.random.fold_in(jax.random.fold_in(key, 6), dim), (blocks,), jnp.float32, least / len(shards), high / len(shards))
        factor_of = factor_of * jnp.repeat(jnp.exp(heights), dims[dim] // blocks).reshape((-1,) + (1,) * (len(dims) - 1 - dim))
    return factor_of


def centred(key, shape, deviation, bound, cuts=(), held_as=jnp.bfloat16):
    drawn = deviation * jax.random.normal(key, shape, jnp.float32)
    if cuts:
        drawn = drawn * shard_levels(key, shape, cuts, -0.22, 0.18)
    return jnp.clip(drawn, -bound, bound).astype(held_as)


def setup_inputs(seed: int = 0) -> dict:
    key_list = jax.random.split(jax.random.key(seed), 12)
    step_hidden = draw_step_hidden(jax.random.fold_in(key_list[11], 71), 0)
    paused_hidden = draw_paused_hidden(jax.random.fold_in(key_list[11], 71), 0)
    ln_gain = jnp.clip(1.0 + 0.18 * jax.random.normal(key_list[2], (D,), jnp.float32), 0.1, 1.9)
    ln_bias = centred(key_list[3], (D,), 0.5, 3.0, ((0, 16),), jnp.float32)
    w_query = draw_w_query(jax.random.fold_in(key_list[11], 71), 0)
    w_keyval = centred(key_list[5], (D, 2, WIDTH), D ** -0.5, 0.0546875, ((0, 16), (2, 32)))
    w_out = centred(key_list[6], (WIDTH, D), HEAD_DIM ** -0.5, 0.5, ((0, 32), (1, 16)))
    cache = centred(key_list[7], (SEQS, 2, CACHE, WIDTH), 1.0, 6.0, ((0, 16), (3, 32)))
    cache_lengths = draw_cache_lengths(jax.random.fold_in(key_list[11], 71), 0)
    partner = jax.random.permutation(key_list[9], N_REP).astype(jnp.int32)
    paused_count = draw_paused_count(jax.random.fold_in(key_list[11], 71), 0)
    return dict(step_hidden=step_hidden, paused_hidden=paused_hidden, ln_gain=ln_gain, ln_bias=ln_bias, w_query=w_query, w_keyval=w_keyval, w_out=w_out, cache=cache, cache_lengths=cache_lengths, partner=partner, paused_count=paused_count)


def layer_norm(values, ln_gain, ln_bias):
    wide = values.astype(jnp.float32)
    center = lax.optimization_barrier(jnp.mean(wide, axis=1, keepdims=True))
    offset = wide - center
    spread = lax.optimization_barrier(jnp.mean(offset * offset, axis=1, keepdims=True))
    return (offset * lax.rsqrt(spread + 1e-05) * ln_gain + ln_bias).astype(jnp.bfloat16)

def attend(query, keys, values, length, own_key, own_value):
    count = keys.shape[0]
    factor = 1.0 / math.sqrt(HEAD_DIM)
    qwide = query.astype(jnp.float32).reshape(HEADS, HEAD_DIM)
    kwide = keys.astype(jnp.float32).reshape(count, HEADS, HEAD_DIM)
    scores = jnp.einsum('hd,chd->hc', qwide, kwide) * factor
    own = lax.optimization_barrier(jnp.sum(qwide * own_key.astype(jnp.float32).reshape(HEADS, HEAD_DIM), axis=1)) * factor
    valid = jnp.arange(count).astype(jnp.int32) < length
    scores = jnp.where(valid[None, :], scores, -jnp.inf)
    whole = jnp.concatenate([scores, own[:, None]], axis=1)
    top = lax.optimization_barrier(jnp.max(whole, axis=1, keepdims=True))
    expo = jnp.exp(whole - top)
    weights = (expo / lax.optimization_barrier(jnp.sum(expo, axis=1, keepdims=True))).astype(jnp.bfloat16)
    weights = lax.optimization_barrier(weights).astype(jnp.float32)
    vwide = jnp.concatenate([values, own_value[None, :]], axis=0).astype(jnp.float32)
    vwide = vwide.reshape(count + 1, HEADS, HEAD_DIM)
    return jnp.einsum('hc,chd->hd', weights, vwide).reshape(WIDTH)

def reference(step_hidden, paused_hidden, ln_gain, ln_bias, w_query, w_keyval, w_out, cache, cache_lengths, partner, paused_count):
    normed_step = layer_norm(step_hidden, ln_gain, ln_bias)
    normed_paused = layer_norm(paused_hidden, ln_gain, ln_bias)
    received = jnp.take(normed_paused.reshape(N_REP, MIG, D), partner, axis=0).reshape(PAUSED, D)
    keyval = jnp.stack([jnp.dot(received, w_keyval[:, 0, :], preferred_element_type=jnp.float32), jnp.dot(received, w_keyval[:, 1, :], preferred_element_type=jnp.float32)], axis=1)
    counts = jnp.take(paused_count, partner)
    live = (jnp.arange(MIG).astype(jnp.int32)[None, :] < counts[:, None]).reshape(PAUSED)
    paused_keyval = jnp.where(live[:, None, None], keyval, 0.0).astype(jnp.bfloat16)
    query = jnp.dot(normed_step, w_query, preferred_element_type=jnp.float32).astype(jnp.bfloat16)
    step_keyval = jnp.stack([jnp.dot(normed_step, w_keyval[:, 0, :], preferred_element_type=jnp.float32), jnp.dot(normed_step, w_keyval[:, 1, :], preferred_element_type=jnp.float32)], axis=1).astype(jnp.bfloat16)
    query = query.reshape(N_REP, NQ, WIDTH)
    step_keyval = step_keyval.reshape(N_REP, NQ, 2, WIDTH)
    resident_query = query[:, :SEQ_DEV].reshape(SEQS, WIDTH)
    resident_own = step_keyval[:, :SEQ_DEV].reshape(SEQS, 2, WIDTH)

    def resident_one(item):
        single, stored, length, own = item
        return attend(single, stored[0], stored[1], length, own[0], own[1])
    resident = lax.map(resident_one, (resident_query, cache, cache_lengths, resident_own))
    grouped = paused_keyval.reshape(N_REP, MIG, 2, WIDTH)

    def migrated_one(item):
        single, stored, length, own = item
        return attend(single, stored[:, 0], stored[:, 1], length, own[0], own[1])
    migrated = lax.map(migrated_one, (query[:, SEQ_DEV], grouped, counts, step_keyval[:, SEQ_DEV]))
    mixed = jnp.concatenate([resident.reshape(N_REP, SEQ_DEV, WIDTH), migrated[:, None, :]], axis=1)
    mixed = mixed.reshape(ROWS, WIDTH).astype(jnp.bfloat16)
    attention_update = jnp.dot(mixed, w_out, preferred_element_type=jnp.float32).astype(jnp.bfloat16)
    return (paused_keyval, attention_update)
```

```python
import math

import jax
import jax.numpy as jnp
from jax import lax
from jax.experimental import pallas as pl
from jax.experimental.pallas import tpu as pltpu
from jax.sharding import PartitionSpec as P

D = 12288
HEAD_DIM = 128
MIG = 112
MESH = pl.DeviceIdType.MESH
F32 = jnp.float32
BF16 = jnp.bfloat16

REP = 16
HEAD = 32
FEATS = D // REP
HALF = MIG // 2
ROWS = 80
NQ = 5
FACTOR = 1.0 / math.sqrt(HEAD_DIM)


def rows_of(shape):
    return lax.broadcasted_iota(jnp.int32, shape, len(shape) - 2)


def lanes_of(shape):
    return lax.broadcasted_iota(jnp.int32, shape, len(shape) - 1)


def wait_bytes(ref, sem):
    pltpu.make_async_copy(ref, ref, sem).wait()


def kernel(
    partner,
    paused_count,
    lengths,
    step_ref,
    paused_ref,
    gain_ref,
    bias_ref,
    w_query_hbm,
    w_keyval_hbm,
    w_out_hbm,
    cache_hbm,
    keyval_out,
    update_out,
    w_all,
    w_out,
    cache,
    stats,
    gathered,
    partial,
    step_send,
    step_recv,
    ring_send,
    ring_recv,
    pair_send,
    pair_recv,
    mixed_all,
    upd_send,
    upd_recv,
    final,
    load_sem,
    stats_sems,
    ag_send,
    ag_recv,
    step_sems,
    ring_ssem,
    ring_rsem,
    pair_ssem,
    pair_rsem,
    mixed_sems,
    upd_sems,
    final_sems,
):
    rep = lax.axis_index("rep")
    head = lax.axis_index("head")
    y, zl = rep // 2, lax.rem(rep, 2)
    core = lax.rem(head, 2)
    chip = head // 2
    zh, x = chip // 4, lax.rem(chip, 4)

    barrier = pltpu.get_barrier_semaphore()

    def greet_rep(d, carry):
        pl.semaphore_signal(
            barrier, inc=1, device_id=(lax.rem(rep + d, REP), head), device_id_type=MESH
        )
        return carry

    def greet_head(d, carry):
        pl.semaphore_signal(
            barrier, inc=1, device_id=(rep, lax.rem(head + d, HEAD)), device_id_type=MESH
        )
        return carry

    lax.fori_loop(1, REP, greet_rep, 0)
    lax.fori_loop(1, HEAD, greet_head, 0)

    loads = [
        pltpu.make_async_copy(w_query_hbm, w_all.at[:, pl.ds(0, 256)], load_sem.at[0]),
        pltpu.make_async_copy(w_keyval_hbm, w_all.at[:, pl.ds(256, 512)], load_sem.at[1]),
        pltpu.make_async_copy(cache_hbm, cache, load_sem.at[2]),
        pltpu.make_async_copy(w_out_hbm, w_out, load_sem.at[3]),
    ]
    for load in loads:
        load.start()

    def all_peers(axis_size, me, sends):
        def body(d, carry):
            sends(lax.rem(me + d, axis_size))
            return carry

        lax.fori_loop(1, axis_size, body, 0)

    def local_stats(values):
        wide = values.astype(F32)
        mean = jnp.sum(wide, axis=1, keepdims=True) / FEATS
        offset = wide - mean
        return mean, jnp.sum(offset * offset, axis=1, keepdims=True)

    def place(pair, lane, rows):
        lanes = lanes_of((rows, 128))
        block = jnp.where(lanes == lane, pair[0], jnp.where(lanes == lane + 1, pair[1], 0.0))
        return jnp.concatenate([block, jnp.zeros((128 - rows, 128), F32)], axis=0)

    packed = place(local_stats(step_ref[...]), 0, ROWS) + place(
        local_stats(paused_ref[...]), 2, HALF
    )
    stats[rep] = jnp.transpose(packed)[:8]

    pl.semaphore_wait(barrier, REP + HEAD - 2)

    def send_stats(peer):
        pltpu.make_async_remote_copy(
            src_ref=stats.at[rep],
            dst_ref=stats.at[rep],
            send_sem=stats_sems.at[0],
            recv_sem=stats_sems.at[1],
            device_id=(peer, head),
            device_id_type=MESH,
        ).start()

    all_peers(REP, rep, send_stats)
    wait_bytes(stats.at[pl.ds(0, REP - 1)], stats_sems.at[1])

    every = stats[...]
    mean = jnp.sum(every, axis=0) / REP
    away = every - mean[None]
    away = jnp.sum(away * away, axis=0)
    sums = mean * REP

    def scale_of(row):
        spread = (sums[row + 1 : row + 2] + FEATS * away[row : row + 1]) / D
        return lax.rsqrt(spread + 1e-05)

    columns = jnp.transpose(
        jnp.concatenate(
            [mean[0:1], scale_of(0), mean[2:3], scale_of(2), jnp.zeros((4, 128), F32)], axis=0
        )
    )

    def normalize(values, lane, rows):
        center = columns[:rows, lane : lane + 1]
        scale = columns[:rows, lane + 1 : lane + 2]
        return ((values.astype(F32) - center) * scale * gain_ref[...] + bias_ref[...]).astype(BF16)

    normed_paused = normalize(paused_ref[...], 2, HALF).astype(F32)
    gathered[head] = jnp.concatenate(
        [normed_paused, jnp.zeros((8, FEATS), F32)], axis=0
    ).astype(BF16)

    def slot(jz, jx, c):
        return (lax.rem(zh + jz + 4, 4) * 4 + lax.rem(x + jx + 4, 4)) * 2 + c

    sent = []

    def pass_on(jz, jx, tz, tx, to_core):
        where = slot(jz, jx, core)
        target = slot(tz, tx, 1 - core if to_core else core)
        copy = pltpu.make_async_remote_copy(
            src_ref=gathered.at[where],
            dst_ref=gathered.at[where],
            send_sem=ag_send.at[len(sent)],
            recv_sem=ag_recv.at[where],
            device_id=(rep, target),
            device_id_type=MESH,
        )
        copy.start()
        sent.append(copy)

    def arrive(where):
        wait_bytes(gathered.at[where], ag_recv.at[where])

    pass_on(0, 0, 1, 0, False)
    pass_on(0, 0, -1, 0, False)
    pass_on(0, 0, 0, 1, False)
    pass_on(0, 0, 0, -1, False)
    pass_on(0, 0, 0, 0, True)

    normed_step = normalize(step_ref[...], 0, ROWS)
    row, col = rows_of((128, ROWS)), lanes_of((128, ROWS))
    spread_rows = jnp.where((row // 8) * NQ + lax.rem(row, 8) == col, 1.0, 0.0)
    spread_rows = jnp.where(lax.rem(row, 8) < NQ, spread_rows, 0.0).astype(BF16)
    padded_step = jnp.dot(spread_rows, normed_step, preferred_element_type=F32).astype(BF16)
    loads[0].wait()
    loads[1].wait()
    step_part = jnp.dot(padded_step, w_all[...], preferred_element_type=F32)
    step_send[...] = step_part.reshape(REP, 8, FEATS)
    step_recv[rep] = step_send[rep]

    def send_step(peer):
        pltpu.make_async_remote_copy(
            src_ref=step_send.at[peer],
            dst_ref=step_recv.at[rep],
            send_sem=step_sems.at[0],
            recv_sem=step_sems.at[1],
            device_id=(peer, head),
            device_id_type=MESH,
        ).start()

    all_peers(REP, rep, send_step)

    for jz, jx in (
        (-1, 0),
        (1, 0),
        (0, -1),
        (0, 1),
        (2, 0),
        (-1, -1),
        (-1, 1),
        (1, -1),
        (1, 1),
        (0, 2),
        (2, -1),
        (2, 1),
        (-1, 2),
        (1, 2),
        (2, 2),
    ):
        arrive(slot(jz, jx, core))
        if jx == 0:
            if jz == -1:
                pass_on(jz, jx, 1, 0, False)
            pass_on(jz, jx, 0, 1, False)
            pass_on(jz, jx, 0, -1, False)
        if jx == -1 and jz in (0, 2):
            pass_on(jz, jx, 0, 1, False)
        if jx == 1 and jz in (-1, 1):
            pass_on(jz, jx, 0, -1, False)
        pass_on(jz, jx, 0, 0, True)

    def arrive_other(i, carry):
        arrive(i * 2 + 1 - core)
        return carry

    lax.fori_loop(0, 16, arrive_other, 0)

    def project(i, carry):
        rows = gathered[pl.ds(i * 8, 8)].reshape(512, FEATS)
        part = jnp.dot(rows, w_all[:, 256:], preferred_element_type=F32).reshape(4, 2, 64, 512)
        for j in range(4):
            partial[i * 4 + j, 0:HALF] = part[j, 0, 0:HALF]
            partial[i * 4 + j, HALF:MIG] = part[j, 1, 0:HALF]
        return carry

    lax.fori_loop(0, 4, project, 0)

    def own_part(to_y, k):
        blocks = []
        for z in range(2):
            group = partner[to_y * 2 + z]
            blocks.append(partial[group, :, k * 256 : (k + 1) * 256])
        return jnp.concatenate(blocks, axis=0)

    def ring_step(way, k, s):
        steps = 4 if way == k else 3
        sign = 1 if way == 0 else -1
        block = own_part(lax.rem(y + sign * (steps - s) + 8, 8), k)
        if s > 0:
            wait_bytes(ring_recv.at[way, k, s - 1], ring_rsem.at[way, k, s - 1])
            block = block + ring_recv[way, k, s - 1].astype(F32)
        ring_send[way, k, s] = block.astype(BF16)
        copy = pltpu.make_async_remote_copy(
            src_ref=ring_send.at[way, k, s],
            dst_ref=ring_recv.at[way, k, s],
            send_sem=ring_ssem.at[way, k, s],
            recv_sem=ring_rsem.at[way, k, s],
            device_id=(lax.rem(y + sign + 8, 8) * 2 + zl, head),
            device_id_type=MESH,
        )
        copy.start()
        sent.append(copy)

    for s in range(4):
        for k in range(2):
            for way in range(2):
                if s < (4 if way == k else 3):
                    ring_step(way, k, s)
        if s == 0:
            wait_bytes(step_recv.at[pl.ds(0, REP - 1)], step_sems.at[1])
            step_qkv = jnp.sum(step_recv[...], axis=0).astype(BF16)
            loads[2].wait()

            def weigh(scores, own, valid):
                scores = jnp.where(valid, scores, -jnp.inf)
                top = jnp.maximum(jnp.max(scores, axis=1, keepdims=True), own)
                expo = jnp.exp(scores - top)
                expo_own = jnp.exp(own - top)
                total = jnp.sum(expo, axis=1, keepdims=True) + expo_own
                return (expo / total).astype(BF16), (expo_own / total).astype(BF16).astype(F32)

            def take(part, h):
                start = part * 256 + h * HEAD_DIM
                return step_qkv[:, start : start + HEAD_DIM]

            def own_score(h):
                return (
                    jnp.sum(take(0, h).astype(F32) * take(1, h).astype(F32), axis=1, keepdims=True)
                    * FACTOR
                )

            def score(query, keys):
                return (
                    lax.dot_general(
                        query, keys, (((1,), (1,)), ((), ())), preferred_element_type=F32
                    )
                    * FACTOR
                )

            resident = []
            row = rows_of((8, 512))
            limit = jnp.zeros((8, 512), jnp.int32)
            for b in range(4):
                limit = jnp.where(row == b, lengths[b], limit)
            valid = lanes_of((8, 512)) < limit
            token = rows_of((8, HEAD_DIM))
            for h in range(2):
                span = slice(h * HEAD_DIM, (h + 1) * HEAD_DIM)
                scores = jnp.zeros((8, 512), F32)
                for b in range(4):
                    scores = jnp.where(row == b, score(take(0, h), cache[b, 0, :, span]), scores)
                weights, weight_own = weigh(scores, own_score(h), valid)
                mixed = jnp.zeros((8, HEAD_DIM), F32)
                for b in range(4):
                    found = jnp.dot(weights, cache[b, 1, :, span], preferred_element_type=F32)
                    mixed = jnp.where(token == b, found, mixed)
                resident.append(mixed + weight_own * take(2, h).astype(F32))

    totals = []
    for k in range(2):
        block = own_part(y, k)
        for way in range(2):
            last = (4 if way == k else 3) - 1
            wait_bytes(ring_recv.at[way, k, last], ring_rsem.at[way, k, last])
            block = block + ring_recv[way, k, last].astype(F32)
        low, high = block[:MIG], block[MIG:]
        totals.append(jnp.where(zl == 0, low, high))
        pair_send[k] = jnp.where(zl == 0, high, low).astype(BF16)
        copy = pltpu.make_async_remote_copy(
            src_ref=pair_send.at[k],
            dst_ref=pair_recv.at[k],
            send_sem=pair_ssem.at[k],
            recv_sem=pair_rsem.at[k],
            device_id=(y * 2 + 1 - zl, head),
            device_id_type=MESH,
        )
        copy.start()
        sent.append(copy)
    live = paused_count[partner[rep]]
    keyval = []
    for k in range(2):
        wait_bytes(pair_recv.at[k], pair_rsem.at[k])
        block = totals[k] + pair_recv[k].astype(F32)
        block = jnp.where(rows_of((MIG, 256)) < live, block, 0.0).astype(BF16)
        keyval_out[k] = block
        keyval.append(block)

    halves = []
    for h in range(2):
        span = slice(h * HEAD_DIM, (h + 1) * HEAD_DIM)
        scores = score(take(0, h), keyval[0][:, span])
        weights, weight_own = weigh(scores, own_score(h), lanes_of((8, MIG)) < live)
        migrated = jnp.dot(weights, keyval[1][:, span], preferred_element_type=F32)
        migrated = migrated + weight_own * take(2, h).astype(F32)
        halves.append(jnp.where(token < 4, resident[h], migrated))
    mixed_all[rep] = jnp.concatenate(halves, axis=1).astype(BF16).astype(F32)

    def send_mixed(peer):
        pltpu.make_async_remote_copy(
            src_ref=mixed_all.at[rep],
            dst_ref=mixed_all.at[rep],
            send_sem=mixed_sems.at[0],
            recv_sem=mixed_sems.at[1],
            device_id=(peer, head),
            device_id_type=MESH,
        ).start()

    all_peers(REP, rep, send_mixed)
    row, col = rows_of((ROWS, 128)), lanes_of((ROWS, 128))
    pack_rows = jnp.where((row // NQ) * 8 + lax.rem(row, NQ) == col, 1.0, 0.0).astype(BF16)
    loads[3].wait()
    wait_bytes(mixed_all.at[pl.ds(0, REP - 1)], mixed_sems.at[1])
    every = mixed_all[...].reshape(128, 256).astype(BF16)
    every = jnp.dot(pack_rows, every, preferred_element_type=F32).astype(BF16)
    update = jnp.dot(every, w_out[...], preferred_element_type=F32).astype(BF16)
    for i in range(5):
        for j in range(6):
            upd_send[i * 6 + j] = update[i * 16 : i * 16 + 16, j * 128 : j * 128 + 128]
    for i in range(30, 32):
        upd_send[i] = jnp.zeros((16, 128), BF16)
    upd_recv[head] = upd_send[head]

    def send_update(peer):
        pltpu.make_async_remote_copy(
            src_ref=upd_send.at[peer],
            dst_ref=upd_recv.at[head],
            send_sem=upd_sems.at[0],
            recv_sem=upd_sems.at[1],
            device_id=(rep, peer),
            device_id_type=MESH,
        ).start()

    all_peers(HEAD, head, send_update)
    wait_bytes(upd_recv.at[pl.ds(0, HEAD - 1)], upd_sems.at[1])
    final[head] = jnp.sum(upd_recv[...].astype(F32), axis=0).astype(BF16)

    def send_final(peer):
        pltpu.make_async_remote_copy(
            src_ref=final.at[head],
            dst_ref=final.at[head],
            send_sem=final_sems.at[0],
            recv_sem=final_sems.at[1],
            device_id=(rep, peer),
            device_id_type=MESH,
        ).start()

    all_peers(HEAD, head, send_final)
    wait_bytes(final.at[pl.ds(0, HEAD - 1)], final_sems.at[1])
    for i in range(5):
        for j in range(6):
            update_out[i * 16 : i * 16 + 16, j * 128 : j * 128 + 128] = final[i * 6 + j]

    for copy in sent:
        copy.wait_send()
    wait_bytes(stats.at[pl.ds(0, REP - 1)], stats_sems.at[0])
    wait_bytes(step_send.at[pl.ds(0, REP - 1)], step_sems.at[0])
    wait_bytes(mixed_all.at[pl.ds(0, REP - 1)], mixed_sems.at[0])
    wait_bytes(upd_send.at[pl.ds(0, HEAD - 1)], upd_sems.at[0])
    wait_bytes(final.at[pl.ds(0, HEAD - 1)], final_sems.at[0])


def on_device(
    step_hidden,
    paused_hidden,
    ln_gain,
    ln_bias,
    w_query,
    w_keyval,
    w_out,
    cache,
    cache_lengths,
    partner,
    paused_count,
):
    vmem = pl.BlockSpec(memory_space=pltpu.VMEM)
    smem = pl.BlockSpec(memory_space=pltpu.SMEM)
    anywhere = pl.BlockSpec(memory_space=pl.ANY)
    dma = pltpu.SemaphoreType.DMA
    keyval, update = pl.pallas_call(
        kernel,
        out_shape=(
            jax.ShapeDtypeStruct((2, MIG, 256), BF16),
            jax.ShapeDtypeStruct((ROWS, FEATS), BF16),
        ),
        in_specs=[smem] * 3 + [vmem] * 4 + [anywhere] * 4,
        out_specs=[vmem] * 2,
        scratch_shapes=[
            pltpu.VMEM((FEATS, 768), BF16),
            pltpu.VMEM((256, FEATS), BF16),
            pltpu.VMEM((4, 2, 512, 256), BF16),
            pltpu.VMEM((REP, 8, 128), F32),
            pltpu.VMEM((HEAD, 64, FEATS), BF16),
            pltpu.VMEM((REP, MIG, 512), F32),
            pltpu.VMEM((REP, 8, FEATS), F32),
            pltpu.VMEM((REP, 8, FEATS), F32),
            pltpu.VMEM((2, 2, 4, 2 * MIG, 256), BF16),
            pltpu.VMEM((2, 2, 4, 2 * MIG, 256), BF16),
            pltpu.VMEM((2, MIG, 256), BF16),
            pltpu.VMEM((2, MIG, 256), BF16),
            pltpu.VMEM((REP, 8, 256), F32),
            pltpu.VMEM((HEAD, 16, 128), BF16),
            pltpu.VMEM((HEAD, 16, 128), BF16),
            pltpu.VMEM((HEAD, 16, 128), BF16),
            dma((4,)),
            dma((2,)),
            dma((32,)),
            dma((HEAD,)),
            dma((2,)),
            dma((2, 2, 4)),
            dma((2, 2, 4)),
            dma((2,)),
            dma((2,)),
            dma((2,)),
            dma((2,)),
            dma((2,)),
        ],
        compiler_params=pltpu.CompilerParams(
            collective_id=0, has_side_effects=True, vmem_limit_bytes=40 * 1024 * 1024
        ),
        name="sublayer",
    )(
        partner,
        paused_count,
        cache_lengths,
        step_hidden,
        paused_hidden,
        ln_gain.reshape(1, -1),
        ln_bias.reshape(1, -1),
        w_query,
        w_keyval.reshape(-1, 512),
        w_out,
        cache,
    )
    return jnp.transpose(keyval, (1, 0, 2)), update


def solution(mesh):
    in_specs = (
        P(None, "rep"),
        P("head", "rep"),
        P("rep"),
        P("rep"),
        P("rep", "head"),
        P("rep", None, "head"),
        P("head", "rep"),
        P("rep", None, None, "head"),
        P("rep"),
        P(),
        P(),
    )
    out_specs = (P("rep", None, "head"), P(None, "rep"))
    return jax.shard_map(
        on_device, mesh=mesh, in_specs=in_specs, out_specs=out_specs, check_vma=False
    )
```

```python
import math

import jax
import jax.numpy as jnp
from jax import lax
from jax.experimental import pallas as pl
from jax.experimental.pallas import tpu as pltpu
from jax.sharding import PartitionSpec as P

D = 12288
HEAD_DIM = 128
MIG = 112
MESH = pl.DeviceIdType.MESH
F32 = jnp.float32
BF16 = jnp.bfloat16

REP = 16
HEAD = 32
FEATS = D // REP
HALF = MIG // 2
PIECE = 32
KEEP = (32, 24)
ROWS = 80
NQ = 5
FACTOR = 1.0 / math.sqrt(HEAD_DIM)


def rows_of(shape):
    return lax.broadcasted_iota(jnp.int32, shape, len(shape) - 2)


def lanes_of(shape):
    return lax.broadcasted_iota(jnp.int32, shape, len(shape) - 1)


def wait_bytes(ref, sem):
    pltpu.make_async_copy(ref, ref, sem).wait()


def push(src, dst, sems, device_id):
    pltpu.make_async_remote_copy(
        src_ref=src,
        dst_ref=dst,
        send_sem=sems.at[0],
        recv_sem=sems.at[1],
        device_id=device_id,
        device_id_type=MESH,
    ).start()


def kernel(
    partner_hbm,
    count_hbm,
    lengths_hbm,
    step_hbm,
    paused_hbm,
    gain_hbm,
    bias_hbm,
    w_query_hbm,
    w_keyval_hbm,
    w_out_hbm,
    cache_hbm,
    keyval_out,
    update_out,
    partner,
    paused_count,
    lengths,
    step_ref,
    paused_ref,
    gain_ref,
    bias_ref,
    w_pairs,
    w_split,
    w_all,
    w_out,
    cache,
    stats,
    stat_all,
    gathered,
    part0,
    part1,
    step_send,
    step_recv,
    ring_send0,
    ring_send1,
    ring_recv0,
    ring_recv1,
    pair_send0,
    pair_send1,
    pair_recv0,
    pair_recv1,
    mixed_res,
    mixed_mig,
    res_swap,
    res_z,
    res_x,
    res_fin,
    mig_swap,
    mig_z,
    mig_x,
    mig_fin,
    load_sem,
    stats_sems,
    statz_sems,
    statx_sems,
    ag_send,
    ag_recv,
    row_send,
    row_recv,
    step_sems,
    ring_ssem,
    ring_rsem,
    pair_ssem,
    pair_rsem,
    mres_sems,
    mmig_sems,
    res_sems,
    mig_sems,
):
    rep = lax.axis_index("rep")
    head = lax.axis_index("head")
    y, zl = rep // 2, lax.rem(rep, 2)
    core = lax.rem(head, 2)
    chip = head // 2
    zh, x = chip // 4, lax.rem(chip, 4)

    def at_head(jz, jx, c):
        return (rep, (lax.rem(zh + jz + 4, 4) * 4 + lax.rem(x + jx + 4, 4)) * 2 + c)

    z_peers = [at_head(j, 0, core) for j in (2, 1, 3)]
    x_peers = [at_head(0, j, core) for j in (2, 1, 3)]
    cross_peers = [at_head(0, j, 1 - core) for j in (2, 1, 3)]
    twin = at_head(0, 0, 1 - core)

    sources = [
        (paused_hbm, paused_ref),
        (step_hbm, step_ref),
        (gain_hbm, gain_ref),
        (bias_hbm, bias_ref),
        (w_keyval_hbm, w_pairs),
        (w_query_hbm, w_all.at[:, pl.ds(0, 256)]),
        (partner_hbm, partner),
        (count_hbm, paused_count),
        (lengths_hbm, lengths),
        (cache_hbm, cache),
        (w_out_hbm, w_out),
    ]
    loads = [
        pltpu.make_async_copy(src, dst, load_sem.at[i]) for i, (src, dst) in enumerate(sources)
    ]
    loads[0].start()

    barrier = pltpu.get_barrier_semaphore()
    for peer in z_peers + x_peers + cross_peers + [twin]:
        pl.semaphore_signal(barrier, inc=1, device_id=peer, device_id_type=MESH)

    def greet_rep(d, carry):
        pl.semaphore_signal(
            barrier, inc=1, device_id=(lax.rem(rep + d, REP), head), device_id_type=MESH
        )
        return carry

    lax.fori_loop(1, REP, greet_rep, 0)
    for load in loads[1:]:
        load.start()

    def to_rep(send):
        def body(d, carry):
            send(lax.rem(rep + d, REP))
            return carry

        lax.fori_loop(1, REP, body, 0)

    own_slot = core * 16 + chip
    loads[0].wait()
    own_rows = paused_ref[...].astype(F32)
    gathered[0, own_slot] = own_rows[:PIECE].astype(BF16)
    gathered[1, own_slot] = jnp.concatenate(
        [own_rows[PIECE:], jnp.zeros((2 * PIECE - HALF, FEATS), F32)], axis=0
    ).astype(BF16)

    pl.semaphore_wait(barrier, REP - 1 + 10)

    def slot_of(jz, jx):
        return core * 16 + lax.rem(zh + jz + 4, 4) * 4 + lax.rem(x + jx + 4, 4)

    def pass_on(p, jz, jx, tz, tx):
        block = gathered.at[p, slot_of(jz, jx)]
        pltpu.make_async_remote_copy(
            src_ref=block,
            dst_ref=block,
            send_sem=ag_send.at[p],
            recv_sem=ag_recv.at[p, slot_of(jz, jx)],
            device_id=at_head(tz, tx, core),
            device_id_type=MESH,
        ).start()

    def row_on(p, jz):
        row = lax.rem(zh + jz + 4, 4)
        block = gathered.at[p, pl.ds(core * 16 + row * 4, 4)]
        pltpu.make_async_remote_copy(
            src_ref=block,
            dst_ref=block,
            send_sem=row_send.at[p],
            recv_sem=row_recv.at[p, row],
            device_id=twin,
            device_id_type=MESH,
        ).start()

    def own_on(p):
        pass_on(p, 0, 0, 1, 0)
        pass_on(p, 0, 0, -1, 0)
        pass_on(p, 0, 0, 0, 1)
        pass_on(p, 0, 0, 0, -1)

    def arrive(p, *places):
        for jz, jx in places:
            where = slot_of(jz, jx)
            wait_bytes(gathered.at[p, where], ag_recv.at[p, where])
            if jx == 0:
                if jz == -1:
                    pass_on(p, jz, jx, 1, 0)
                pass_on(p, jz, jx, 0, 1)
                pass_on(p, jz, jx, 0, -1)
            if jx == -1 and jz in (0, 2):
                pass_on(p, jz, jx, 0, 1)
            if jx == 1 and jz in (-1, 1):
                pass_on(p, jz, jx, 0, -1)
            if jx == 2:
                row_on(p, jz)

    own_on(0)
    own_on(1)

    def local_stats(wide):
        mean = jnp.sum(wide, axis=1, keepdims=True) / FEATS
        offset = wide - mean
        return mean, jnp.sum(offset * offset, axis=1, keepdims=True)

    def place(pair, lane, rows):
        lanes = lanes_of((rows, 128))
        block = jnp.where(lanes == lane, pair[0], jnp.where(lanes == lane + 1, pair[1], 0.0))
        return jnp.concatenate([block, jnp.zeros((128 - rows, 128), F32)], axis=0)

    loads[1].wait()
    packed = place(local_stats(step_ref[...].astype(F32)), 0, ROWS) + place(
        local_stats(own_rows), 2, HALF
    )
    stats[rep] = jnp.transpose(packed)[:8]
    to_rep(lambda peer: push(stats.at[rep], stats.at[rep], stats_sems, (peer, head)))

    for i in range(2, 9):
        loads[i].wait()

    def split(i, carry):
        wide = w_pairs[pl.ds(i * 32, 32)].reshape(64, 256).astype(F32)
        w_split[pl.ds(0, 64)] = wide[:, :128]
        w_split[pl.ds(64, 64)] = wide[:, 128:]
        for k in range(2):
            for j in range(2):
                start = 256 + k * 256 + j * 128
                w_all[pl.ds(i * 32, 32), start : start + 128] = w_split[
                    pl.ds(k + 64 * j, 32, stride=2), :
                ].astype(BF16)
        return carry

    lax.fori_loop(0, FEATS // 32, split, 0)

    arrive(0, (0, -1), (0, 1), (-1, 0), (1, 0))
    arrive(1, (0, -1), (0, 1), (-1, 0), (1, 0))

    wait_bytes(stats.at[pl.ds(0, REP - 1)], stats_sems.at[1])
    every = stats[...]
    mean = jnp.sum(every, axis=0) / REP
    away = every - mean[None]
    away = jnp.sum(away * away, axis=0)
    sums = mean * REP

    def scale_of(row):
        spread = (sums[row + 1 : row + 2] + FEATS * away[row : row + 1]) / D
        return lax.rsqrt(spread + 1e-05)

    lines = jnp.concatenate(
        [mean[0:1], scale_of(0), mean[2:3], scale_of(2), jnp.zeros((4, 128), F32)], axis=0
    )
    stat_slot = core * 16 + x * 4 + zh
    stat_all[stat_slot] = lines
    for peer in z_peers:
        push(stat_all.at[stat_slot], stat_all.at[stat_slot], statz_sems, peer)

    gain = gain_ref[...].reshape(1, FEATS)
    bias = bias_ref[...].reshape(1, FEATS)

    def normalize(wide, columns, lane):
        center = columns[:, lane : lane + 1]
        scale = columns[:, lane + 1 : lane + 2]
        return ((wide - center) * scale * gain + bias).astype(BF16)

    arrive(0, (2, 0), (0, 2), (-1, -1), (-1, 1), (1, -1), (1, 1))

    normed_step = normalize(step_ref[...].astype(F32), jnp.transpose(lines)[:ROWS], 0)
    row, col = rows_of((128, ROWS)), lanes_of((128, ROWS))
    spread_rows = jnp.where((row // 8) * NQ + lax.rem(row, 8) == col, 1.0, 0.0)
    spread_rows = jnp.where(lax.rem(row, 8) < NQ, spread_rows, 0.0).astype(BF16)
    padded_step = jnp.dot(spread_rows, normed_step, preferred_element_type=F32).astype(BF16)
    step_part = jnp.dot(padded_step, w_all[...], preferred_element_type=F32)
    step_send[...] = step_part.reshape(REP, 8, FEATS)
    step_recv[rep] = step_send[rep]

    wait_bytes(stat_all.at[pl.ds(0, 3)], statz_sems.at[1])
    stat_line = stat_all.at[pl.ds(core * 16 + x * 4, 4)]
    for peer in x_peers + cross_peers + [twin]:
        push(stat_line, stat_line, statx_sems, peer)

    to_rep(lambda peer: push(step_send.at[peer], step_recv.at[rep], step_sems, (peer, head)))

    arrive(1, (2, 0), (0, 2), (-1, -1), (-1, 1), (1, -1), (1, 1))
    arrive(0, (2, -1), (2, 1), (-1, 2), (1, 2), (2, 2))

    parts = (part0, part1)

    def project(p):
        def body(i, carry):
            rows = []
            for j in range(8):
                lines = stat_all[(i // 2) * 16 + (j % 4) * 4 + lax.rem(i, 2) * 2 + j // 4]
                columns = jnp.transpose(lines)[p * PIECE : (p + 1) * PIECE]
                rows.append(normalize(gathered[p, i * 8 + j].astype(F32), columns, 2))
            rows = jnp.concatenate(rows, axis=0)
            found = jnp.dot(rows, w_all[:, 256:], preferred_element_type=F32)
            found = found.reshape(8, PIECE, 512)
            parts[p][i // 2, pl.ds(lax.rem(i, 2) * 8, 8)] = found[:, : KEEP[p]]
            return carry

        for r in range(4):
            wait_bytes(gathered.at[p, pl.ds(0, 4)], row_recv.at[p, r])
        lax.fori_loop(0, 4, body, 0)

    ring_send, ring_recv = (ring_send0, ring_send1), (ring_recv0, ring_recv1)

    def own_part(p, to_y, k):
        blocks = []
        for z in range(2):
            group = partner[to_y * 2 + z]
            for c in range(2):
                blocks.append(parts[p][c, group, :, k * 256 : (k + 1) * 256])
        return jnp.concatenate(blocks, axis=0)

    def ring_step(p, s):
        for k in range(2):
            for way in range(2):
                steps = 4 if way == k else 3
                if s >= steps:
                    continue
                sign = 1 if way == 0 else -1
                here = (way * 2 + k) * 4 + s
                block = own_part(p, lax.rem(y + sign * (steps - s) + 8, 8), k)
                if s > 0:
                    wait_bytes(ring_recv[p].at[here - 1], ring_rsem.at[p, here - 1])
                    block = block + ring_recv[p][here - 1].astype(F32)
                ring_send[p][here] = block.astype(BF16)
                pltpu.make_async_remote_copy(
                    src_ref=ring_send[p].at[here],
                    dst_ref=ring_recv[p].at[here],
                    send_sem=ring_ssem.at[p, here],
                    recv_sem=ring_rsem.at[p, here],
                    device_id=(lax.rem(y + sign + 8, 8) * 2 + zl, head),
                    device_id_type=MESH,
                ).start()

    pair_send, pair_recv = (pair_send0, pair_send1), (pair_recv0, pair_recv1)

    def ring_end(p):
        totals = []
        for k in range(2):
            block = own_part(p, y, k)
            for way in range(2):
                last = (way * 2 + k) * 4 + (4 if way == k else 3) - 1
                wait_bytes(ring_recv[p].at[last], ring_rsem.at[p, last])
                block = block + ring_recv[p][last].astype(F32)
            low, high = block[: 2 * KEEP[p]], block[2 * KEEP[p] :]
            totals.append(jnp.where(zl == 0, low, high))
            pair_send[p][k] = jnp.where(zl == 0, high, low).astype(BF16)
            pltpu.make_async_remote_copy(
                src_ref=pair_send[p].at[k],
                dst_ref=pair_recv[p].at[k],
                send_sem=pair_ssem.at[p, k],
                recv_sem=pair_rsem.at[p, k],
                device_id=(y * 2 + 1 - zl, head),
                device_id_type=MESH,
            ).start()
        return totals

    def weigh(scores, own, valid):
        scores = jnp.where(valid, scores, -jnp.inf)
        top = jnp.maximum(jnp.max(scores, axis=1, keepdims=True), own)
        expo = jnp.exp(scores - top)
        expo_own = jnp.exp(own - top)
        total = jnp.sum(expo, axis=1, keepdims=True) + expo_own
        return (expo / total).astype(BF16), (expo_own / total).astype(BF16).astype(F32)

    def score(query, keys):
        dims = (((1,), (1,)), ((), ()))
        return lax.dot_general(query, keys, dims, preferred_element_type=F32) * FACTOR

    def take(part, h):
        start = part * 256 + h * HEAD_DIM
        return step_qkv[:, start : start + HEAD_DIM]

    def own_score(h):
        products = take(0, h).astype(F32) * take(1, h).astype(F32)
        return jnp.sum(products, axis=1, keepdims=True) * FACTOR

    def swap_halves(update, swap, sems):
        left, right = update[:, :384], update[:, 384:]
        swap[0] = jnp.where(core == 0, right, left).astype(BF16)
        push(swap.at[0], swap.at[1], sems.at[0], twin)
        return jnp.where(core == 0, left, right)

    def spread(block, buffer, me, peers, sems):
        buffer[me] = block.astype(BF16)
        for peer in peers:
            push(buffer.at[me], buffer.at[me], sems, peer)

    def sum_over_z(mine, swap, buffer, sems):
        wait_bytes(swap.at[1], sems.at[0, 1])
        spread(mine + swap[1].astype(F32), buffer, zh, z_peers, sems.at[1])

    def sum_over_x(buffer, wide, sems):
        wait_bytes(buffer.at[pl.ds(0, 3)], sems.at[1, 1])
        spread(jnp.sum(buffer[...].astype(F32), axis=0), wide, x, x_peers, sems.at[2])

    def join(buffer, fin, sems):
        wait_bytes(buffer.at[pl.ds(0, 3)], sems.at[2, 1])
        fin[core] = jnp.sum(buffer[...].astype(F32), axis=0).astype(BF16)
        push(fin.at[core], fin.at[core], sems.at[3], twin)

    def joined(fin, sems):
        wait_bytes(fin.at[0], sems.at[3, 1])
        return jnp.concatenate([fin[0], fin[1]], axis=1)

    def drained(swap, buffer, wide, fin, sems):
        wait_bytes(swap.at[0], sems.at[0, 0])
        wait_bytes(buffer.at[pl.ds(0, 3)], sems.at[1, 0])
        wait_bytes(wide.at[pl.ds(0, 3)], sems.at[2, 0])
        wait_bytes(fin.at[0], sems.at[3, 0])

    wait_bytes(stat_all.at[pl.ds(0, 28)], statx_sems.at[1])
    project(0)
    ring_step(0, 0)
    arrive(1, (2, -1), (2, 1), (-1, 2), (1, 2), (2, 2))
    ring_step(0, 1)
    project(1)
    ring_step(1, 0)
    ring_step(0, 2)

    wait_bytes(step_recv.at[pl.ds(0, REP - 1)], step_sems.at[1])
    step_qkv = jnp.sum(step_recv[...], axis=0).astype(BF16)
    loads[9].wait()
    row = rows_of((8, 512))
    limit = jnp.zeros((8, 512), jnp.int32)
    for b in range(4):
        limit = jnp.where(row == b, lengths[b], limit)
    valid = lanes_of((8, 512)) < limit
    token = rows_of((8, HEAD_DIM))
    halves = []
    for h in range(2):
        span = slice(h * HEAD_DIM, (h + 1) * HEAD_DIM)
        scores = jnp.zeros((8, 512), F32)
        for b in range(4):
            scores = jnp.where(row == b, score(take(0, h), cache[b, 0, :, span]), scores)
        weights, weight_own = weigh(scores, own_score(h), valid)
        mixed = jnp.zeros((8, HEAD_DIM), F32)
        for b in range(4):
            found = jnp.dot(weights, cache[b, 1, :, span], preferred_element_type=F32)
            mixed = jnp.where(token == b, found, mixed)
        halves.append(mixed + weight_own * take(2, h).astype(F32))
    mixed_res[rep] = jnp.concatenate(halves, axis=1).astype(BF16).astype(F32)
    to_rep(lambda peer: push(mixed_res.at[rep], mixed_res.at[rep], mres_sems, (peer, head)))

    ring_step(1, 1)
    ring_step(0, 3)

    wait_bytes(mixed_res.at[pl.ds(0, REP - 1)], mres_sems.at[1])
    loads[10].wait()
    row, col = rows_of((64, 128)), lanes_of((64, 128))
    pack_rows = jnp.where((row // 4) * 8 + lax.rem(row, 4) == col, 1.0, 0.0).astype(BF16)
    every = mixed_res[...].reshape(128, 256).astype(BF16)
    every = jnp.dot(pack_rows, every, preferred_element_type=F32).astype(BF16)
    update = jnp.dot(every, w_out[...], preferred_element_type=F32)
    mine = swap_halves(update, res_swap, res_sems)

    ring_step(1, 2)
    totals0 = ring_end(0)
    sum_over_z(mine, res_swap, res_z, res_sems)
    ring_step(1, 3)
    sum_over_x(res_z, res_x, res_sems)
    totals1 = ring_end(1)
    join(res_x, res_fin, res_sems)

    live = paused_count[partner[rep]]
    keyval = []
    for k in range(2):
        blocks = []
        for p, totals in enumerate((totals0, totals1)):
            wait_bytes(pair_recv[p].at[k], pair_rsem.at[p, k])
            blocks.append(totals[k] + pair_recv[p][k].astype(F32))
        first, second = blocks
        block = jnp.concatenate(
            [first[: KEEP[0]], second[: KEEP[1]], first[KEEP[0] :], second[KEEP[1] :]], axis=0
        )
        block = jnp.where(rows_of((MIG, 256)) < live, block, 0.0).astype(BF16)
        keyval_out[k] = block
        keyval.append(block)

    halves = []
    for h in range(2):
        span = slice(h * HEAD_DIM, (h + 1) * HEAD_DIM)
        scores = score(take(0, h), keyval[0][:, span])
        weights, weight_own = weigh(scores, own_score(h), lanes_of((8, MIG)) < live)
        migrated = jnp.dot(weights, keyval[1][:, span], preferred_element_type=F32)
        migrated = migrated + weight_own * take(2, h).astype(F32)
        halves.append(migrated[4:5])
    halves.append(jnp.zeros((6, HEAD_DIM), F32))
    mixed_mig[rep] = jnp.concatenate(halves, axis=0).astype(BF16).astype(F32)
    to_rep(lambda peer: push(mixed_mig.at[rep], mixed_mig.at[rep], mmig_sems, (peer, head)))

    resident = joined(res_fin, res_sems)
    row, col = rows_of((ROWS, 64)), lanes_of((ROWS, 64))
    spread_rows = jnp.where((row // NQ) * 4 + lax.rem(row, NQ) == col, 1.0, 0.0)
    spread_rows = jnp.where(lax.rem(row, NQ) < 4, spread_rows, 0.0).astype(BF16)
    resident = jnp.dot(spread_rows, resident, preferred_element_type=F32)

    wait_bytes(mixed_mig.at[pl.ds(0, REP - 1)], mmig_sems.at[1])
    every = mixed_mig[...].reshape(128, HEAD_DIM).astype(BF16)
    row, col = rows_of((16, 128)), lanes_of((16, 128))
    update = jnp.zeros((16, FEATS), F32)
    for h in range(2):
        pick = jnp.where(row * 8 + h == col, 1.0, 0.0).astype(BF16)
        rows = jnp.dot(pick, every, preferred_element_type=F32).astype(BF16)
        update = update + jnp.dot(
            rows, w_out[h * HEAD_DIM : (h + 1) * HEAD_DIM, :], preferred_element_type=F32
        )
    mine = swap_halves(update, mig_swap, mig_sems)
    sum_over_z(mine, mig_swap, mig_z, mig_sems)
    sum_over_x(mig_z, mig_x, mig_sems)
    join(mig_x, mig_fin, mig_sems)
    migrated = joined(mig_fin, mig_sems)
    row, col = rows_of((ROWS, 16)), lanes_of((ROWS, 16))
    spread_rows = jnp.where(col * NQ + 4 == row, 1.0, 0.0).astype(BF16)
    migrated = jnp.dot(spread_rows, migrated, preferred_element_type=F32)
    update_out[...] = (resident + migrated).astype(BF16)

    wait_bytes(stats.at[pl.ds(0, REP - 1)], stats_sems.at[0])
    wait_bytes(stat_all.at[pl.ds(0, 3)], statz_sems.at[0])
    wait_bytes(stat_all.at[pl.ds(0, 28)], statx_sems.at[0])
    wait_bytes(step_send.at[pl.ds(0, REP - 1)], step_sems.at[0])
    wait_bytes(mixed_res.at[pl.ds(0, REP - 1)], mres_sems.at[0])
    wait_bytes(mixed_mig.at[pl.ds(0, REP - 1)], mmig_sems.at[0])
    for p in range(2):
        wait_bytes(gathered.at[p, pl.ds(0, 15)], ag_send.at[p])
        wait_bytes(gathered.at[p, pl.ds(0, 16)], row_send.at[p])
        for k in range(2):
            wait_bytes(pair_send[p].at[k], pair_ssem.at[p, k])
            for way in range(2):
                for s in range(4 if way == k else 3):
                    here = (way * 2 + k) * 4 + s
                    wait_bytes(ring_send[p].at[here], ring_ssem.at[p, here])
    drained(res_swap, res_z, res_x, res_fin, res_sems)
    drained(mig_swap, mig_z, mig_x, mig_fin, mig_sems)


def on_device(
    step_hidden,
    paused_hidden,
    ln_gain,
    ln_bias,
    w_query,
    w_keyval,
    w_out,
    cache,
    cache_lengths,
    partner,
    paused_count,
):
    vmem = pl.BlockSpec(memory_space=pltpu.VMEM)
    anywhere = pl.BlockSpec(memory_space=pltpu.HBM)
    dma = pltpu.SemaphoreType.DMA
    ring = [pltpu.VMEM((16, 4 * keep, 256), BF16) for keep in KEEP]
    pair = [pltpu.VMEM((2, 2 * keep, 256), BF16) for keep in KEEP]

    def reduction(rows):
        return [
            pltpu.VMEM((2, rows, 384), BF16),
            pltpu.VMEM((4, rows, 384), BF16),
            pltpu.VMEM((4, rows, 384), BF16),
            pltpu.VMEM((2, rows, 384), BF16),
        ]

    keyval, update = pl.pallas_call(
        kernel,
        out_shape=(
            jax.ShapeDtypeStruct((2, MIG, 256), BF16),
            jax.ShapeDtypeStruct((ROWS, FEATS), BF16),
        ),
        in_specs=[anywhere] * 11,
        out_specs=[vmem] * 2,
        scratch_shapes=[
            pltpu.SMEM((REP,), jnp.int32),
            pltpu.SMEM((REP,), jnp.int32),
            pltpu.SMEM((4,), jnp.int32),
            pltpu.VMEM((ROWS, FEATS), BF16),
            pltpu.VMEM((HALF, FEATS), BF16),
            pltpu.VMEM((FEATS,), F32),
            pltpu.VMEM((FEATS,), F32),
            pltpu.VMEM((FEATS, 2, 256), BF16),
            pltpu.VMEM((128, 128), F32),
            pltpu.VMEM((FEATS, 768), BF16),
            pltpu.VMEM((256, FEATS), BF16),
            pltpu.VMEM((4, 2, 512, 256), BF16),
            pltpu.VMEM((REP, 8, 128), F32),
            pltpu.VMEM((HEAD, 8, 128), F32),
            pltpu.VMEM((2, HEAD, PIECE, FEATS), BF16),
            pltpu.VMEM((2, REP, KEEP[0], 512), F32),
            pltpu.VMEM((2, REP, KEEP[1], 512), F32),
            pltpu.VMEM((REP, 8, FEATS), F32),
            pltpu.VMEM((REP, 8, FEATS), F32),
        ]
        + ring * 2
        + pair * 2
        + [pltpu.VMEM((REP, 8, 256), F32), pltpu.VMEM((REP, 8, 128), F32)]
        + reduction(64)
        + reduction(16)
        + [
            dma((11,)),
            dma((2,)),
            dma((2,)),
            dma((2,)),
            dma((2,)),
            dma((2, HEAD)),
            dma((2,)),
            dma((2, 4)),
            dma((2,)),
            dma((2, 16)),
            dma((2, 16)),
            dma((2, 2)),
            dma((2, 2)),
            dma((2,)),
            dma((2,)),
            dma((4, 2)),
            dma((4, 2)),
        ],
        compiler_params=pltpu.CompilerParams(
            collective_id=0, has_side_effects=True, vmem_limit_bytes=60 * 1024 * 1024
        ),
        name="sublayer",
    )(
        partner,
        paused_count,
        cache_lengths,
        step_hidden,
        paused_hidden,
        ln_gain,
        ln_bias,
        w_query,
        w_keyval,
        w_out,
        cache,
    )
    return jnp.transpose(keyval, (1, 0, 2)), update


def solution(mesh):
    in_specs = (
        P(None, "rep"),
        P("head", "rep"),
        P("rep"),
        P("rep"),
        P("rep", "head"),
        P("rep", None, "head"),
        P("head", "rep"),
        P("rep", None, None, "head"),
        P("rep"),
        P(),
        P(),
    )
    out_specs = (P("rep", None, "head"), P(None, "rep"))
    return jax.shard_map(
        on_device, mesh=mesh, in_specs=in_specs, out_specs=out_specs, check_vma=False
    )
```

```python
import math

import jax
import jax.numpy as jnp
from jax import lax
from jax.experimental import pallas as pl
from jax.experimental.pallas import tpu as pltpu
from jax.sharding import PartitionSpec as P

D = 12288
HEAD_DIM = 128
MIG = 112
MESH = pl.DeviceIdType.MESH
F32 = jnp.float32
BF16 = jnp.bfloat16

REP = 16
HEAD = 32
FEATS = D // REP
HALF = MIG // 2
KEEP = (32, 24)
ROWS = 80
NQ = 5
FACTOR = 1.0 / math.sqrt(HEAD_DIM)


def rows_of(shape):
    return lax.broadcasted_iota(jnp.int32, shape, len(shape) - 2)


def lanes_of(shape):
    return lax.broadcasted_iota(jnp.int32, shape, len(shape) - 1)


def wait_bytes(ref, sem):
    pltpu.make_async_copy(ref, ref, sem).wait()


def push(src, dst, sems, device_id):
    pltpu.make_async_remote_copy(
        src_ref=src,
        dst_ref=dst,
        send_sem=sems.at[0],
        recv_sem=sems.at[1],
        device_id=device_id,
        device_id_type=MESH,
    ).start()


def kernel(
    partner_hbm,
    count_hbm,
    lengths_hbm,
    step_hbm,
    paused_hbm,
    gain_hbm,
    bias_hbm,
    w_query_hbm,
    w_keyval_hbm,
    w_out_hbm,
    cache_hbm,
    keyval_out,
    update_out,
    partner,
    paused_count,
    lengths,
    step_ref,
    paused_ref,
    gain_ref,
    bias_ref,
    w_pairs,
    w_split,
    w_all,
    w_out,
    cache,
    stats,
    stat_all,
    gathered0,
    gathered1,
    part0,
    part1,
    step_send,
    step_recv,
    ring_send0,
    ring_send1,
    ring_recv0,
    ring_recv1,
    pair_send0,
    pair_send1,
    pair_recv0,
    pair_recv1,
    mixed_res,
    mixed_mig,
    res_swap,
    res_z,
    res_x,
    res_fin,
    mig_swap,
    mig_z,
    mig_x,
    mig_fin,
    load_sem,
    stats_sems,
    statz_sems,
    statx_sems,
    ag_send,
    ag_recv,
    row_send,
    row_recv,
    step_sems,
    ring_ssem,
    ring_rsem,
    pair_ssem,
    pair_rsem,
    mres_sems,
    mmig_sems,
    res_sems,
    mig_sems,
):
    rep = lax.axis_index("rep")
    head = lax.axis_index("head")
    y, zl = rep // 2, lax.rem(rep, 2)
    core = lax.rem(head, 2)
    chip = head // 2
    zh, x = chip // 4, lax.rem(chip, 4)

    def at_head(jz, jx, c):
        return (rep, (lax.rem(zh + jz + 4, 4) * 4 + lax.rem(x + jx + 4, 4)) * 2 + c)

    z_peers = [at_head(j, 0, core) for j in (2, 1, 3)]
    x_peers = [at_head(0, j, core) for j in (2, 1, 3)]
    cross_peers = [at_head(0, j, 1 - core) for j in (2, 1, 3)]
    twin = at_head(0, 0, 1 - core)

    sources = [
        (paused_hbm, paused_ref),
        (step_hbm, step_ref),
        (gain_hbm, gain_ref),
        (bias_hbm, bias_ref),
        (w_keyval_hbm, w_pairs),
        (w_query_hbm, w_all.at[:, pl.ds(0, 256)]),
        (partner_hbm, partner),
        (count_hbm, paused_count),
        (lengths_hbm, lengths),
        (cache_hbm, cache),
        (w_out_hbm, w_out),
    ]
    loads = [
        pltpu.make_async_copy(src, dst, load_sem.at[i]) for i, (src, dst) in enumerate(sources)
    ]
    loads[0].start()

    barrier = pltpu.get_barrier_semaphore()
    for peer in z_peers + x_peers + cross_peers + [twin]:
        pl.semaphore_signal(barrier, inc=1, device_id=peer, device_id_type=MESH)

    def greet_rep(d, carry):
        pl.semaphore_signal(
            barrier, inc=1, device_id=(lax.rem(rep + d, REP), head), device_id_type=MESH
        )
        return carry

    lax.fori_loop(1, REP, greet_rep, 0)
    for load in loads[1:]:
        load.start()

    def to_rep(send):
        def body(d, carry):
            send(lax.rem(rep + d, REP))
            return carry

        lax.fori_loop(1, REP, body, 0)

    gathered = (gathered0, gathered1)
    own_slot = core * 16 + chip
    loads[0].wait()
    own_rows = paused_ref[...].astype(F32)
    gathered0[own_slot] = own_rows[: KEEP[0]].astype(BF16)
    gathered1[own_slot] = jnp.concatenate(
        [
            own_rows[32:48, :384],
            own_rows[32:48, 384:],
            own_rows[48:56, :384],
            own_rows[48:56, 384:],
        ],
        axis=0,
    ).astype(BF16)

    pl.semaphore_wait(barrier, REP - 1 + 10)

    def slot_of(jz, jx):
        return core * 16 + lax.rem(zh + jz + 4, 4) * 4 + lax.rem(x + jx + 4, 4)

    def pass_on(p, jz, jx, tz, tx):
        block = gathered[p].at[slot_of(jz, jx)]
        pltpu.make_async_remote_copy(
            src_ref=block,
            dst_ref=block,
            send_sem=ag_send.at[p],
            recv_sem=ag_recv.at[p, slot_of(jz, jx)],
            device_id=at_head(tz, tx, core),
            device_id_type=MESH,
        ).start()

    def row_on(p, jz):
        row = lax.rem(zh + jz + 4, 4)
        block = gathered[p].at[pl.ds(core * 16 + row * 4, 4)]
        pltpu.make_async_remote_copy(
            src_ref=block,
            dst_ref=block,
            send_sem=row_send.at[p],
            recv_sem=row_recv.at[p, row],
            device_id=twin,
            device_id_type=MESH,
        ).start()

    def own_on(p):
        pass_on(p, 0, 0, 1, 0)
        pass_on(p, 0, 0, -1, 0)
        pass_on(p, 0, 0, 0, 1)
        pass_on(p, 0, 0, 0, -1)

    def arrive(p, *places):
        for jz, jx in places:
            where = slot_of(jz, jx)
            wait_bytes(gathered[p].at[where], ag_recv.at[p, where])
            if jx == 0:
                if jz == -1:
                    pass_on(p, jz, jx, 1, 0)
                pass_on(p, jz, jx, 0, 1)
                pass_on(p, jz, jx, 0, -1)
            if jx == -1 and jz in (0, 2):
                pass_on(p, jz, jx, 0, 1)
            if jx == 1 and jz in (-1, 1):
                pass_on(p, jz, jx, 0, -1)
            if jx == 2:
                row_on(p, jz)

    own_on(0)
    own_on(1)

    def local_stats(wide):
        mean = jnp.sum(wide, axis=1, keepdims=True) / FEATS
        offset = wide - mean
        return mean, jnp.sum(offset * offset, axis=1, keepdims=True)

    def place(pair, lane, rows):
        lanes = lanes_of((rows, 128))
        block = jnp.where(lanes == lane, pair[0], jnp.where(lanes == lane + 1, pair[1], 0.0))
        return jnp.concatenate([block, jnp.zeros((128 - rows, 128), F32)], axis=0)

    loads[1].wait()
    packed = place(local_stats(step_ref[...].astype(F32)), 0, ROWS) + place(
        local_stats(own_rows), 2, HALF
    )
    stats[rep] = jnp.transpose(packed)[:8]
    to_rep(lambda peer: push(stats.at[rep], stats.at[rep], stats_sems, (peer, head)))

    for i in range(2, 9):
        loads[i].wait()

    def split(i, carry):
        wide = w_pairs[pl.ds(i * 32, 32)].reshape(64, 256).astype(F32)
        w_split[pl.ds(0, 64)] = wide[:, :128]
        w_split[pl.ds(64, 64)] = wide[:, 128:]
        for k in range(2):
            for j in range(2):
                start = 256 + k * 256 + j * 128
                w_all[pl.ds(i * 32, 32), start : start + 128] = w_split[
                    pl.ds(k + 64 * j, 32, stride=2), :
                ].astype(BF16)
        return carry

    lax.fori_loop(0, FEATS // 32, split, 0)

    arrive(0, (0, -1), (0, 1), (-1, 0), (1, 0))
    arrive(1, (0, -1), (0, 1), (-1, 0), (1, 0))

    wait_bytes(stats.at[pl.ds(0, REP - 1)], stats_sems.at[1])
    every = stats[...]
    mean = jnp.sum(every, axis=0) / REP
    away = every - mean[None]
    away = jnp.sum(away * away, axis=0)
    sums = mean * REP

    def scale_of(row):
        spread = (sums[row + 1 : row + 2] + FEATS * away[row : row + 1]) / D
        return lax.rsqrt(spread + 1e-05)

    lines = jnp.concatenate(
        [mean[0:1], scale_of(0), mean[2:3], scale_of(2), jnp.zeros((4, 128), F32)], axis=0
    )
    stat_slot = core * 16 + x * 4 + zh
    stat_all[stat_slot] = lines
    for peer in z_peers:
        push(stat_all.at[stat_slot], stat_all.at[stat_slot], statz_sems, peer)

    gain = gain_ref[...].reshape(1, FEATS)
    bias = bias_ref[...].reshape(1, FEATS)

    def normalize(wide, columns, lane):
        center = columns[:, lane : lane + 1]
        scale = columns[:, lane + 1 : lane + 2]
        return ((wide - center) * scale * gain + bias).astype(BF16)

    arrive(0, (2, 0), (0, 2), (-1, -1), (-1, 1), (1, -1), (1, 1))
    arrive(1, (2, 0), (0, 2), (-1, -1), (-1, 1), (1, -1), (1, 1))
    wait_bytes(stat_all.at[pl.ds(0, 3)], statz_sems.at[1])
    stat_line = stat_all.at[pl.ds(core * 16 + x * 4, 4)]
    for peer in x_peers + cross_peers + [twin]:
        push(stat_line, stat_line, statx_sems, peer)

    normed_step = normalize(step_ref[...].astype(F32), jnp.transpose(lines)[:ROWS], 0)
    row, col = rows_of((128, ROWS)), lanes_of((128, ROWS))
    spread_rows = jnp.where((row // 8) * NQ + lax.rem(row, 8) == col, 1.0, 0.0)
    spread_rows = jnp.where(lax.rem(row, 8) < NQ, spread_rows, 0.0).astype(BF16)
    padded_step = jnp.dot(spread_rows, normed_step, preferred_element_type=F32).astype(BF16)
    step_part = jnp.dot(padded_step, w_all[...], preferred_element_type=F32)
    step_send[...] = step_part.reshape(REP, 8, FEATS)
    step_recv[rep] = step_send[rep]

    to_rep(lambda peer: push(step_send.at[peer], step_recv.at[rep], step_sems, (peer, head)))

    arrive(0, (2, -1), (2, 1), (-1, 2), (1, 2), (2, 2))
    arrive(1, (2, -1), (2, 1))

    parts = (part0, part1)

    def project(p):
        def body(i, carry):
            rows = []
            for j in range(8):
                lines = stat_all[(i // 2) * 16 + (j % 4) * 4 + lax.rem(i, 2) * 2 + j // 4]
                columns = jnp.transpose(lines)[p * KEEP[0] : p * KEEP[0] + KEEP[p]]
                block = gathered[p][i * 8 + j].astype(F32)
                if p == 1:
                    left = jnp.concatenate([block[0:16], block[32:40]], axis=0)
                    right = jnp.concatenate([block[16:32], block[40:48]], axis=0)
                    block = jnp.concatenate([left, right], axis=1)
                rows.append(normalize(block, columns, 2).astype(F32))
            rows = jnp.concatenate(rows, axis=0).astype(BF16)
            found = jnp.dot(rows, w_all[:, 256:], preferred_element_type=F32)
            found = found.reshape(8, KEEP[p], 512)
            parts[p][i // 2, pl.ds(lax.rem(i, 2) * 8, 8)] = found
            return carry

        for r in range(4):
            wait_bytes(gathered[p].at[pl.ds(0, 4)], row_recv.at[p, r])
        lax.fori_loop(0, 4, body, 0)

    ring_send, ring_recv = (ring_send0, ring_send1), (ring_recv0, ring_recv1)

    def own_part(p, to_y, k):
        blocks = []
        for z in range(2):
            group = partner[to_y * 2 + z]
            for c in range(2):
                blocks.append(parts[p][c, group, :, k * 256 : (k + 1) * 256])
        return jnp.concatenate(blocks, axis=0)

    def ring_step(p, s):
        for k in range(2):
            for way in range(2):
                steps = 4 if way == k else 3
                if s >= steps:
                    continue
                sign = 1 if way == 0 else -1
                here = (way * 2 + k) * 4 + s
                block = own_part(p, lax.rem(y + sign * (steps - s) + 8, 8), k)
                if s > 0:
                    wait_bytes(ring_recv[p].at[here - 1], ring_rsem.at[p, here - 1])
                    block = block + ring_recv[p][here - 1].astype(F32)
                ring_send[p][here] = block.astype(BF16)
                pltpu.make_async_remote_copy(
                    src_ref=ring_send[p].at[here],
                    dst_ref=ring_recv[p].at[here],
                    send_sem=ring_ssem.at[p, here],
                    recv_sem=ring_rsem.at[p, here],
                    device_id=(lax.rem(y + sign + 8, 8) * 2 + zl, head),
                    device_id_type=MESH,
                ).start()

    pair_send, pair_recv = (pair_send0, pair_send1), (pair_recv0, pair_recv1)

    def ring_end(p):
        totals = []
        for k in range(2):
            block = own_part(p, y, k)
            for way in range(2):
                last = (way * 2 + k) * 4 + (4 if way == k else 3) - 1
                wait_bytes(ring_recv[p].at[last], ring_rsem.at[p, last])
                block = block + ring_recv[p][last].astype(F32)
            low, high = block[: 2 * KEEP[p]], block[2 * KEEP[p] :]
            totals.append(jnp.where(zl == 0, low, high))
            pair_send[p][k] = jnp.where(zl == 0, high, low).astype(BF16)
            pltpu.make_async_remote_copy(
                src_ref=pair_send[p].at[k],
                dst_ref=pair_recv[p].at[k],
                send_sem=pair_ssem.at[p, k],
                recv_sem=pair_rsem.at[p, k],
                device_id=(y * 2 + 1 - zl, head),
                device_id_type=MESH,
            ).start()
        return totals

    def weigh(scores, own, valid):
        scores = jnp.where(valid, scores, -jnp.inf)
        top = jnp.maximum(jnp.max(scores, axis=1, keepdims=True), own)
        expo = jnp.exp(scores - top)
        expo_own = jnp.exp(own - top)
        total = jnp.sum(expo, axis=1, keepdims=True) + expo_own
        return (expo / total).astype(BF16), (expo_own / total).astype(BF16).astype(F32)

    def score(query, keys):
        dims = (((1,), (1,)), ((), ()))
        return lax.dot_general(query, keys, dims, preferred_element_type=F32) * FACTOR

    def take(part, h):
        start = part * 256 + h * HEAD_DIM
        return step_qkv[:, start : start + HEAD_DIM]

    def own_score(h):
        products = take(0, h).astype(F32) * take(1, h).astype(F32)
        return jnp.sum(products, axis=1, keepdims=True) * FACTOR

    def swap_halves(update, swap, sems):
        left, right = update[:, :384], update[:, 384:]
        swap[0] = jnp.where(core == 0, right, left).astype(BF16)
        push(swap.at[0], swap.at[1], sems.at[0], twin)
        return jnp.where(core == 0, left, right)

    def spread(block, buffer, me, peers, sems):
        buffer[me] = block.astype(BF16)
        for peer in peers:
            push(buffer.at[me], buffer.at[me], sems, peer)

    def sum_over_z(mine, swap, buffer, sems):
        wait_bytes(swap.at[1], sems.at[0, 1])
        spread(mine + swap[1].astype(F32), buffer, zh, z_peers, sems.at[1])

    def sum_over_x(buffer, wide, sems):
        wait_bytes(buffer.at[pl.ds(0, 3)], sems.at[1, 1])
        spread(jnp.sum(buffer[...].astype(F32), axis=0), wide, x, x_peers, sems.at[2])

    def join(buffer, fin, sems):
        wait_bytes(buffer.at[pl.ds(0, 3)], sems.at[2, 1])
        fin[core] = jnp.sum(buffer[...].astype(F32), axis=0).astype(BF16)
        push(fin.at[core], fin.at[core], sems.at[3], twin)

    def joined(fin, sems):
        wait_bytes(fin.at[0], sems.at[3, 1])
        return jnp.concatenate([fin[0], fin[1]], axis=1)

    def drained(swap, buffer, wide, fin, sems):
        wait_bytes(swap.at[0], sems.at[0, 0])
        wait_bytes(buffer.at[pl.ds(0, 3)], sems.at[1, 0])
        wait_bytes(wide.at[pl.ds(0, 3)], sems.at[2, 0])
        wait_bytes(fin.at[0], sems.at[3, 0])

    wait_bytes(stat_all.at[pl.ds(0, 28)], statx_sems.at[1])
    project(0)
    ring_step(0, 0)

    wait_bytes(step_recv.at[pl.ds(0, REP - 1)], step_sems.at[1])
    step_qkv = jnp.sum(step_recv[...], axis=0).astype(BF16)
    loads[9].wait()
    token = rows_of((8, HEAD_DIM))

    def resident_weights(h):
        row = rows_of((8, 512))
        limit = jnp.zeros((8, 512), jnp.int32)
        for b in range(4):
            limit = jnp.where(row == b, lengths[b], limit)
        scores = jnp.zeros((8, 512), F32)
        for b in range(4):
            keys = cache[b, 0, :, h * HEAD_DIM : (h + 1) * HEAD_DIM]
            scores = jnp.where(row == b, score(take(0, h), keys), scores)
        return weigh(scores, own_score(h), lanes_of((8, 512)) < limit)

    def resident_mix(h, weights, weight_own):
        mixed = jnp.zeros((8, HEAD_DIM), F32)
        for b in range(4):
            values = cache[b, 1, :, h * HEAD_DIM : (h + 1) * HEAD_DIM]
            found = jnp.dot(weights, values, preferred_element_type=F32)
            mixed = jnp.where(token == b, found, mixed)
        mixed = mixed + weight_own * take(2, h).astype(F32)
        mixed_res[rep, :, h * HEAD_DIM : (h + 1) * HEAD_DIM] = mixed.astype(BF16).astype(F32)

    arrive(1, (-1, 2), (1, 2), (2, 2))
    first = resident_weights(0)
    ring_step(0, 1)
    project(1)
    ring_step(1, 0)
    ring_step(0, 2)
    resident_mix(0, *first)
    second = resident_weights(1)
    ring_step(1, 1)
    resident_mix(1, *second)
    to_rep(lambda peer: push(mixed_res.at[rep], mixed_res.at[rep], mres_sems, (peer, head)))
    ring_step(0, 3)
    ring_step(1, 2)
    totals0 = ring_end(0)

    wait_bytes(mixed_res.at[pl.ds(0, REP - 1)], mres_sems.at[1])
    loads[10].wait()
    row, col = rows_of((64, 128)), lanes_of((64, 128))
    pack_rows = jnp.where((row // 4) * 8 + lax.rem(row, 4) == col, 1.0, 0.0).astype(BF16)
    every = mixed_res[...].reshape(128, 256).astype(BF16)
    every = jnp.dot(pack_rows, every, preferred_element_type=F32).astype(BF16)
    update = jnp.dot(every, w_out[...], preferred_element_type=F32)
    mine = swap_halves(update, res_swap, res_sems)

    ring_step(1, 3)
    sum_over_z(mine, res_swap, res_z, res_sems)
    totals1 = ring_end(1)

    live = paused_count[partner[rep]]
    keyval = []
    for k in range(2):
        blocks = []
        for p, totals in enumerate((totals0, totals1)):
            wait_bytes(pair_recv[p].at[k], pair_rsem.at[p, k])
            blocks.append(totals[k] + pair_recv[p][k].astype(F32))
        first, second = blocks
        block = jnp.concatenate(
            [first[: KEEP[0]], second[: KEEP[1]], first[KEEP[0] :], second[KEEP[1] :]], axis=0
        )
        block = jnp.where(rows_of((MIG, 256)) < live, block, 0.0).astype(BF16)
        keyval_out[k] = block
        keyval.append(block)

    halves = []
    for h in range(2):
        span = slice(h * HEAD_DIM, (h + 1) * HEAD_DIM)
        scores = score(take(0, h), keyval[0][:, span])
        weights, weight_own = weigh(scores, own_score(h), lanes_of((8, MIG)) < live)
        migrated = jnp.dot(weights, keyval[1][:, span], preferred_element_type=F32)
        migrated = migrated + weight_own * take(2, h).astype(F32)
        halves.append(migrated[4:5])
    halves.append(jnp.zeros((6, HEAD_DIM), F32))
    mixed_mig[rep] = jnp.concatenate(halves, axis=0).astype(BF16).astype(F32)
    to_rep(lambda peer: push(mixed_mig.at[rep], mixed_mig.at[rep], mmig_sems, (peer, head)))

    sum_over_x(res_z, res_x, res_sems)
    join(res_x, res_fin, res_sems)

    wait_bytes(mixed_mig.at[pl.ds(0, REP - 1)], mmig_sems.at[1])
    every = mixed_mig[...].reshape(128, HEAD_DIM).astype(BF16)
    row, col = rows_of((16, 128)), lanes_of((16, 128))
    update = jnp.zeros((16, FEATS), F32)
    for h in range(2):
        pick = jnp.where(row * 8 + h == col, 1.0, 0.0).astype(BF16)
        rows = jnp.dot(pick, every, preferred_element_type=F32).astype(BF16)
        update = update + jnp.dot(
            rows, w_out[h * HEAD_DIM : (h + 1) * HEAD_DIM, :], preferred_element_type=F32
        )
    mine = swap_halves(update, mig_swap, mig_sems)
    sum_over_z(mine, mig_swap, mig_z, mig_sems)

    resident = joined(res_fin, res_sems)
    row, col = rows_of((ROWS, 64)), lanes_of((ROWS, 64))
    spread_rows = jnp.where((row // NQ) * 4 + lax.rem(row, NQ) == col, 1.0, 0.0)
    spread_rows = jnp.where(lax.rem(row, NQ) < 4, spread_rows, 0.0).astype(BF16)
    resident = jnp.dot(spread_rows, resident, preferred_element_type=F32)

    sum_over_x(mig_z, mig_x, mig_sems)
    join(mig_x, mig_fin, mig_sems)
    migrated = joined(mig_fin, mig_sems)
    row, col = rows_of((ROWS, 16)), lanes_of((ROWS, 16))
    spread_rows = jnp.where(col * NQ + 4 == row, 1.0, 0.0).astype(BF16)
    migrated = jnp.dot(spread_rows, migrated, preferred_element_type=F32)
    update_out[...] = (resident + migrated).astype(BF16)

    wait_bytes(stats.at[pl.ds(0, REP - 1)], stats_sems.at[0])
    wait_bytes(stat_all.at[pl.ds(0, 3)], statz_sems.at[0])
    wait_bytes(stat_all.at[pl.ds(0, 28)], statx_sems.at[0])
    wait_bytes(step_send.at[pl.ds(0, REP - 1)], step_sems.at[0])
    wait_bytes(mixed_res.at[pl.ds(0, REP - 1)], mres_sems.at[0])
    wait_bytes(mixed_mig.at[pl.ds(0, REP - 1)], mmig_sems.at[0])
    for p in range(2):
        wait_bytes(gathered[p].at[pl.ds(0, 15)], ag_send.at[p])
        wait_bytes(gathered[p].at[pl.ds(0, 16)], row_send.at[p])
        for k in range(2):
            wait_bytes(pair_send[p].at[k], pair_ssem.at[p, k])
            for way in range(2):
                for s in range(4 if way == k else 3):
                    here = (way * 2 + k) * 4 + s
                    wait_bytes(ring_send[p].at[here], ring_ssem.at[p, here])
    drained(res_swap, res_z, res_x, res_fin, res_sems)
    drained(mig_swap, mig_z, mig_x, mig_fin, mig_sems)


def on_device(
    step_hidden,
    paused_hidden,
    ln_gain,
    ln_bias,
    w_query,
    w_keyval,
    w_out,
    cache,
    cache_lengths,
    partner,
    paused_count,
):
    vmem = pl.BlockSpec(memory_space=pltpu.VMEM)
    anywhere = pl.BlockSpec(memory_space=pltpu.HBM)
    dma = pltpu.SemaphoreType.DMA
    ring = [pltpu.VMEM((16, 4 * keep, 256), BF16) for keep in KEEP]
    pair = [pltpu.VMEM((2, 2 * keep, 256), BF16) for keep in KEEP]

    def reduction(rows):
        return [
            pltpu.VMEM((2, rows, 384), BF16),
            pltpu.VMEM((4, rows, 384), BF16),
            pltpu.VMEM((4, rows, 384), BF16),
            pltpu.VMEM((2, rows, 384), BF16),
        ]

    keyval, update = pl.pallas_call(
        kernel,
        out_shape=(
            jax.ShapeDtypeStruct((2, MIG, 256), BF16),
            jax.ShapeDtypeStruct((ROWS, FEATS), BF16),
        ),
        in_specs=[anywhere] * 11,
        out_specs=[vmem] * 2,
        scratch_shapes=[
            pltpu.SMEM((REP,), jnp.int32),
            pltpu.SMEM((REP,), jnp.int32),
            pltpu.SMEM((4,), jnp.int32),
            pltpu.VMEM((ROWS, FEATS), BF16),
            pltpu.VMEM((HALF, FEATS), BF16),
            pltpu.VMEM((FEATS,), F32),
            pltpu.VMEM((FEATS,), F32),
            pltpu.VMEM((FEATS, 2, 256), BF16),
            pltpu.VMEM((128, 128), F32),
            pltpu.VMEM((FEATS, 768), BF16),
            pltpu.VMEM((256, FEATS), BF16),
            pltpu.VMEM((4, 2, 512, 256), BF16),
            pltpu.VMEM((REP, 8, 128), F32),
            pltpu.VMEM((HEAD, 8, 128), F32),
            pltpu.VMEM((HEAD, KEEP[0], FEATS), BF16),
            pltpu.VMEM((HEAD, 2 * KEEP[1], FEATS // 2), BF16),
            pltpu.VMEM((2, REP, KEEP[0], 512), F32),
            pltpu.VMEM((2, REP, KEEP[1], 512), F32),
            pltpu.VMEM((REP, 8, FEATS), F32),
            pltpu.VMEM((REP, 8, FEATS), F32),
        ]
        + ring * 2
        + pair * 2
        + [pltpu.VMEM((REP, 8, 256), F32), pltpu.VMEM((REP, 8, 128), F32)]
        + reduction(64)
        + reduction(16)
        + [
            dma((11,)),
            dma((2,)),
            dma((2,)),
            dma((2,)),
            dma((2,)),
            dma((2, HEAD)),
            dma((2,)),
            dma((2, 4)),
            dma((2,)),
            dma((2, 16)),
            dma((2, 16)),
            dma((2, 2)),
            dma((2, 2)),
            dma((2,)),
            dma((2,)),
            dma((4, 2)),
            dma((4, 2)),
        ],
        compiler_params=pltpu.CompilerParams(
            collective_id=0, has_side_effects=True, vmem_limit_bytes=60 * 1024 * 1024
        ),
        name="sublayer",
    )(
        partner,
        paused_count,
        cache_lengths,
        step_hidden,
        paused_hidden,
        ln_gain,
        ln_bias,
        w_query,
        w_keyval,
        w_out,
        cache,
    )
    return jnp.transpose(keyval, (1, 0, 2)), update


def solution(mesh):
    in_specs = (
        P(None, "rep"),
        P("head", "rep"),
        P("rep"),
        P("rep"),
        P("rep", "head"),
        P("rep", None, "head"),
        P("head", "rep"),
        P("rep", None, None, "head"),
        P("rep"),
        P(),
        P(),
    )
    out_specs = (P("rep", None, "head"), P(None, "rep"))
    return jax.shard_map(
        on_device, mesh=mesh, in_specs=in_specs, out_specs=out_specs, check_vma=False
    )
```
